128 devices in a mesh: row: 8 (over z_hi, x), col: 16 (over z_lo, y, core).
Axes of the slice: x: 4, y: 4, z: 4 (z_hi: 2, z_lo: 2; z = z_hi * 2 + z_lo), core: 2. Of those that a mesh axis runs over, the one named last changes fastest.
Arguments:
- ainv: float32 [24576, 24576], P('row', 'col'), may hold values from -0.0390625 to 0.0390625
- lpanel: float32 [24576, 1024], P(('row', 'col')), may hold values from -0.6 to 0.6
- dinv: float32 [1024, 512], P(('row', 'col')), may hold values from -6 to 6
- lmask: int32 [384, 2], P(('row', 'col')), may hold values 0 or 1
- hrows: float32 [24576, 1024], P(('row', 'col')), may hold values from -6 to 6
- hmask: int32 [384, 2], P(('row', 'col')), may hold values 0 or 1
- pole_weight: float32 [1], replicated, may hold values from 0.5 to 2
Outputs:
- offdiag: float32 [24576, 1024], P(('row', 'col'))
- diaginv: float32 [1024, 512], P(('row', 'col'))
- energy: float32 [24576], P(('row', 'col'))
The draws below stay inside these ranges and needn't reach their ends.
All inputs are finite; a program needn't handle non-finite values. No bound on the sum of `lmask` or of `hmask` on one device may be relied on, other than what follows from the above.
Results may differ from the reference program's by a relative error of at most 0.00024.
Values sent between devices are 32-bit elements; how exact they have to be, the bound alone decides.
No kernel may reach another device: no remote copies, remote signals or barrier semaphores. Data moves between devices by JAX's collectives and lax.ppermute only.
A program may use at most 128 MiB of HBM per device.

```python
import jax
import jax.numpy as jnp
from jax import lax

NC = 24576
SN = 512
BLK = 64
W = 1024
NB = 384


def plant(values, key, low, largest):
    index_at = [jax.random.randint(jax.random.fold_in(key, axis), (), 0, length) for axis, length in enumerate(values.shape)]
    longest = values.shape.index(max(values.shape))
    beside = index_at[:longest] + [(index_at[longest] + 1) % values.shape[longest]] + index_at[longest + 1:]
    return values.at[tuple(index_at)].set(low).at[tuple(beside)].set(largest)


def steps_of(rng, shape, split, least, high):
    factor_of = 1.0
    for axis_at, parts in split:
        steps = jax.random.uniform(jax.random.fold_in(jax.random.fold_in(rng, 6), axis_at), (parts,), jnp.float32, least / len(split), high / len(split))
        factor_of = factor_of * jnp.repeat(jnp.exp(steps), shape[axis_at] // parts).reshape((-1,) + (1,) * (len(shape) - 1 - axis_at))
    return factor_of


def gaussian(own_key, dims, spread, limit, shards=(), held_as=jnp.bfloat16):
    array = jax.random.normal(own_key, dims, jnp.float32) * spread
    if len(shards) > 0:
        array = steps_of(own_key, dims, shards, -0.22, 0.18) * array
    return jnp.clip(array, min=-limit, max=limit).astype(held_as)


def setup_inputs(seed: int = 0) -> dict:
    streams_of = jax.random.split(jax.random.key(seed), 8)
    ainv = gaussian(streams_of[0], (NC, NC), NC ** -0.5, 0.0390625, ((0, 8), (1, 16)), jnp.float32)
    lpanel = gaussian(streams_of[1], (NC, W), 0.08, 0.6, ((0, 128),), jnp.float32)
    dinv = gaussian(streams_of[2], (W, SN), 1.0, 6.0, ((0, 128),), jnp.float32)
    lmask = plant((jax.random.randint(streams_of[3], (NB, 2), 0, 2) < 1).astype(jnp.int32), jax.random.fold_in(streams_of[3], 1), 0, 1)
    hrows = gaussian(streams_of[4], (NC, W), 1.0, 6.0, ((0, 128),), jnp.float32)
    hmask = plant((jax.random.randint(streams_of[5], (NB, 2), 0, 3) < 2).astype(jnp.int32), jax.random.fold_in(streams_of[5], 1), 0, 1)
    pole_weight = jnp.clip(jax.random.uniform(streams_of[6], (1,), jnp.float32, 0.5, 2.0), 0.5, 2.0)
    return {"ainv": ainv, "lpanel": lpanel, "dinv": dinv, "lmask": lmask, "hrows": hrows, "hmask": hmask, "pole_weight": pole_weight}


def expand_mask(mask):
    full = jnp.broadcast_to(mask.astype(jnp.float32)[:, None, :, None], (NB, BLK, 2, SN))
    return full.reshape(NC, W)


def reference(ainv, lpanel, dinv, lmask, hrows, hmask, pole_weight):
    pattern = expand_mask(lmask)
    lmasked = lpanel * pattern
    ycol = jnp.dot(ainv, lmasked, precision=lax.Precision.HIGHEST, preferred_element_type=jnp.float32)
    offdiag = -ycol * pattern
    left = lmasked.reshape(NC, 2, SN)
    right = ycol.reshape(NC, 2, SN)
    blocks = jnp.einsum("rsa,rsb->sab", left, right, precision=lax.Precision.HIGHEST)
    diaginv = dinv + blocks.reshape(W, SN)
    hpattern = expand_mask(hmask)
    energy = pole_weight[0] * jnp.sum(hrows * hpattern * offdiag, axis=1)
    return offdiag, diaginv, energy
```

```python
import functools

import jax
import jax.numpy as jnp
from jax import lax
from jax.experimental import pallas as pl
from jax.experimental.pallas import tpu as pltpu
from jax.sharding import Mesh
from jax.sharding import PartitionSpec as P

AXES = ("zh", "x", "zl", "y", "core")
SIZES = (2, 4, 2, 4, 2)


def shift(array, axis, by):
    size = lax.axis_size(axis)
    return lax.ppermute(array, axis, [(i, (i + by) % size) for i in range(size)])


def to_slabs(array):
    pairs = []
    for zh in range(2):
        for x in range(4):
            for zl in range(2):
                for y in range(4):
                    for core in range(2):
                        source = (((zh * 4 + x) * 2 + zl) * 4 + y) * 2 + core
                        target = (((core * 4 + y) * 2 + zh) * 4 + x) * 2 + zl
                        pairs.append((source, target))
    return lax.ppermute(array, AXES, pairs)


def split(value):
    high = value.astype(jnp.bfloat16)
    low = (value - high.astype(jnp.float32)).astype(jnp.bfloat16)
    return high, low


def product_kernel(where, a_ref, *refs):
    pieces, out_ref, high_ref, low_ref = refs[:8], refs[8], refs[9], refs[10]
    rows = pieces[0].shape[0]

    @pl.when((pl.program_id(0) == 0) & (pl.program_id(1) == 0))
    def _():
        for other in range(2):
            for by in range(4):
                place = lax.rem(where[1] + by, 4) * 2 + jnp.bitwise_xor(where[0], other)
                at = pl.ds(pl.multiple_of(place * rows, 64), rows)
                high, low = split(pieces[other * 4 + by][...])
                high_ref[at, :] = high
                low_ref[at, :] = low

    tiles, tile_rows, depth = a_ref.shape[1], a_ref.shape[3], a_ref.shape[4]
    a_high, a_low = split(a_ref[...].reshape(tiles * tile_rows, depth))
    dot = functools.partial(jnp.dot, preferred_element_type=jnp.float32)
    total = dot(a_low, high_ref[...]) + dot(a_high, low_ref[...]) + dot(a_high, high_ref[...])
    for tile in range(tiles):
        owner = pl.program_id(1) * tiles + tile
        by = lax.rem(owner - where[3] + 4, 4)
        out_ref[0, by] = total[tile * tile_rows : (tile + 1) * tile_rows]


def product(ainv, pieces, where, other_core):
    rows, width = pieces[0].shape
    depth = ainv.shape[1]
    tiles = 2
    blocks = ainv.reshape(2, 4, 2, rows, depth)

    def a_map(dz, part, where):
        return (
            jnp.bitwise_xor(where[2], dz),
            part,
            jnp.bitwise_xor(where[4], other_core),
            0,
            0,
        )

    flops = 2 * 8 * rows * depth * width * 3
    return pl.pallas_call(
        product_kernel,
        grid_spec=pltpu.PrefetchScalarGridSpec(
            num_scalar_prefetch=1,
            grid=(2, 4 // tiles),
            in_specs=[pl.BlockSpec((1, tiles, 1, rows, depth), a_map)]
            + [pl.BlockSpec((rows, width), lambda *_: (0, 0))] * 8,
            out_specs=pl.BlockSpec((1, 4, rows, width), lambda dz, part, where: (dz, 0, 0, 0)),
            scratch_shapes=[pltpu.VMEM((8 * rows, width), jnp.bfloat16)] * 2,
        ),
        out_shape=jax.ShapeDtypeStruct((2, 4, rows, width), jnp.float32),
        compiler_params=pltpu.CompilerParams(vmem_limit_bytes=44 * 1024 * 1024),
        cost_estimate=pl.CostEstimate(
            flops=flops, bytes_accessed=4 * (8 * rows * (depth + 2 * width)), transcendentals=0
        ),
    )(where, blocks, *pieces)


def gather_slab(piece):
    across = shift(piece, "zh", 1)
    from_left, from_right = shift(piece, "x", 1), shift(piece, "x", -1)
    across_left, across_right = shift(across, "x", 1), shift(across, "x", -1)
    opposite = shift(from_left, "x", 1)
    across_opposite = shift(across_right, "x", -1)
    return (
        piece,
        from_right,
        opposite,
        from_left,
        across,
        across_right,
        across_opposite,
        across_left,
    )


def reduce_to_owner(kept, came):
    part = lambda dz, by: kept[dz, by] + came[dz, by]
    up_far = shift(part(0, 2), "y", 1)
    down_far = shift(part(1, 2), "y", -1)
    up_second = shift(part(1, 1), "y", 1)
    down_first = shift(part(0, 3), "y", -1)
    up_first = shift(part(0, 1) + up_far, "y", 1)
    down_second = shift(part(1, 3) + down_far, "y", -1)
    second = part(1, 0) + up_second + down_second
    across = shift(second, "zl", 1)
    return part(0, 0) + up_first + down_first + across


def sum_diag(terms, index):
    at = lambda array, axis, i: lax.dynamic_index_in_dim(array, i, axis, keepdims=False)
    terms = at(terms, 4, index["core"]) + shift(at(terms, 4, 1 - index["core"]), "core", 1)
    for axis, dim in (("y", 3), ("x", 1)):
        total = at(terms, dim, index[axis])
        for by in (1, 3, 2):
            total = total + shift(at(terms, dim, (index[axis] + by) % 4), axis, by)
        terms = total
    own_high, own_low = terms[index["zh"]], terms[1 - index["zh"]]
    own = own_high[index["zl"]]
    near = shift(own_high[1 - index["zl"]], "zl", 1)
    far = shift(own_low[index["zl"]], "zh", 1)
    pairs = [(i, 3 - i) for i in range(4)]
    both = lax.ppermute(own_low[1 - index["zl"]], ("zh", "zl"), pairs)
    return own + near + far + both


def expand_local(mask, block_rows, supernode):
    count = mask.shape[0]
    full = jnp.broadcast_to(
        mask.astype(jnp.float32)[:, None, :, None], (count, block_rows, 2, supernode)
    )
    return full.reshape(count * block_rows, 2 * supernode)


def local(ainv, lpanel, dinv, lmask, hrows, hmask, pole_weight):
    rows_local = lpanel.shape[0]
    supernode = lpanel.shape[1] // 2
    block_rows = rows_local // lmask.shape[0]
    index = {axis: lax.axis_index(axis) for axis in AXES}
    where = jnp.stack([index[axis] for axis in AXES]).astype(jnp.int32)
    pattern = expand_local(lmask, block_rows, supernode)
    lmasked = lpanel * pattern
    owned, terms = [], []
    halves = [lmasked[:, :supernode], lmasked[:, supernode:]]
    for half in halves:
        pieces = gather_slab(to_slabs(half))
        came = shift(product(ainv, pieces, where, 1), "core", 1)
        kept = product(ainv, pieces, where, 0)
        mine = reduce_to_owner(kept, came)
        owned.append(mine)
        terms.append(
            lax.dot_general(
                half,
                mine,
                (((0,), (0,)), ((), ())),
                precision=lax.Precision.HIGHEST,
                preferred_element_type=jnp.float32,
            )
        )
    diag_rows = dinv.shape[0]
    diag = jnp.stack(terms).reshape(*SIZES, diag_rows, supernode)
    diaginv = dinv + sum_diag(diag, index)
    offdiag = -jnp.concatenate(owned, axis=1) * pattern
    hpattern = expand_local(hmask, block_rows, supernode)
    energy = pole_weight[0] * jnp.sum(hrows * hpattern * offdiag, axis=1)
    return (offdiag, diaginv, energy)


def solution(mesh):
    split_mesh = Mesh(mesh.devices.reshape(*SIZES), AXES)
    rows = P(AXES, None)
    return jax.shard_map(
        local,
        mesh=split_mesh,
        in_specs=(P(("zh", "x"), ("zl", "y", "core")), rows, rows, rows, rows, rows, P()),
        out_specs=(rows, rows, P(AXES)),
        check_vma=False,
    )
```

```python
import functools

import jax
import jax.numpy as jnp
from jax import lax
from jax.experimental import pallas as pl
from jax.experimental.pallas import tpu as pltpu
from jax.sharding import Mesh
from jax.sharding import PartitionSpec as P

AXES = ("zh", "x", "zl", "y", "core")
SIZES = (2, 4, 2, 4, 2)


def shift(array, axis, by):
    size = lax.axis_size(axis)
    return lax.ppermute(array, axis, [(i, (i + by) % size) for i in range(size)])


def to_slabs(array):
    pairs = []
    for zh in range(2):
        for x in range(4):
            for zl in range(2):
                for y in range(4):
                    for core in range(2):
                        source = (((zh * 4 + x) * 2 + zl) * 4 + y) * 2 + core
                        to_x = (x + y % 2 * 2 + core) % 4
                        target = (((y // 2 * 4 + to_x) * 2 + zh) * 4 + x) * 2 + zl
                        pairs.append((source, target))
    return lax.ppermute(array, AXES, pairs)


def split(value):
    high = value.astype(jnp.bfloat16)
    low = (value - high.astype(jnp.float32)).astype(jnp.bfloat16)
    return high, low


def load_pieces(where, pieces, columns, high_ref, low_ref):
    rows = pieces[0].shape[0]
    start = lambda by: lax.rem(where[1] + by - where[3] + 4, 4) * rows
    places = (start(0), start(1), start(3), start(2), start(2) + rows // 2)
    for piece, place in zip(pieces, places):
        at = pl.ds(pl.multiple_of(place, 32), piece.shape[0])
        high_ref[at, :], low_ref[at, :] = split(piece[:, columns])


def three_products(a, high_ref, low_ref):
    high, low = split(a)
    dot = functools.partial(jnp.dot, preferred_element_type=jnp.float32)
    return dot(low, high_ref[...]) + dot(high, low_ref[...]) + dot(high, high_ref[...])


def near_kernel(where, a_ref, *refs):
    pieces, out_ref, high_ref, low_ref = refs[:5], *refs[5:]

    @pl.when(pl.program_id(0) == 0)
    def _():
        load_pieces(where, pieces, slice(None), high_ref, low_ref)

    out_ref[...] = three_products(a_ref[...], high_ref, low_ref)


def near_product(ainv, pieces, where):
    total, depth = ainv.shape
    rows, width = pieces[0].shape
    tile = 2 * rows
    return pl.pallas_call(
        near_kernel,
        grid_spec=pltpu.PrefetchScalarGridSpec(
            num_scalar_prefetch=1,
            grid=(total // tile,),
            in_specs=[pl.BlockSpec((tile, depth // 2), lambda i, where: (i, where[0]))]
            + [pl.BlockSpec(memory_space=pltpu.VMEM)] * 5,
            out_specs=pl.BlockSpec((tile, width), lambda i, where: (i, 0)),
            scratch_shapes=[pltpu.VMEM((depth // 2, width), jnp.bfloat16)] * 2,
        ),
        out_shape=jax.ShapeDtypeStruct((total, width), jnp.float32),
        compiler_params=pltpu.CompilerParams(vmem_limit_bytes=36 * 1024 * 1024),
        cost_estimate=pl.CostEstimate(
            flops=3 * total * depth * width,
            bytes_accessed=4 * total * (depth // 2 + width),
            transcendentals=0,
        ),
    )(where, ainv, *pieces)


def far_kernel(columns, where, a_ref, near_ref, *refs):
    pieces, given_ref, kept_ref, high_ref, low_ref = refs[:5], *refs[5:]
    half, part = pl.program_id(0), pl.program_id(2)

    @pl.when((half == 0) & (pl.program_id(1) == 0) & (part == 0))
    def _():
        load_pieces(where, pieces, columns, high_ref, low_ref)

    tiles, tile_rows, depth = a_ref.shape[1], a_ref.shape[3], a_ref.shape[4]
    total = three_products(a_ref[...].reshape(tiles * tile_rows, depth), high_ref, low_ref)
    total = total + near_ref[...].reshape(total.shape)
    for which, out_ref in enumerate((given_ref, kept_ref)):

        @pl.when(half == which)
        def _():
            for tile in range(tiles):
                by = lax.rem(part * tiles + tile - where[3] + 4, 4)
                out_ref[0, by] = total[tile * tile_rows : (tile + 1) * tile_rows]


def far_product(ainv, near, pieces, where, supernode):
    total, depth = ainv.shape
    rows, width = pieces[0].shape[0], pieces[0].shape[1] // 2
    tiles = 2

    def rows_of(half, dz, part, where):
        core = jnp.bitwise_xor(where[4], 1 - half)
        return jnp.bitwise_xor(where[2], dz), part, core, 0

    def a_map(half, dz, part, where):
        return *rows_of(half, dz, part, where), 1 - where[0]

    def near_map(half, dz, part, where):
        return *rows_of(half, dz, part, where), supernode

    def given_map(half, dz, part, where):
        return jnp.maximum(half, dz), 0, 0, 0

    def kept_map(half, dz, part, where):
        return half * dz, 0, 0, 0

    columns = slice(supernode * width, (supernode + 1) * width)
    return pl.pallas_call(
        functools.partial(far_kernel, columns),
        grid_spec=pltpu.PrefetchScalarGridSpec(
            num_scalar_prefetch=1,
            grid=(2, 2, 4 // tiles),
            in_specs=[
                pl.BlockSpec((1, tiles, 1, rows, depth // 2), a_map),
                pl.BlockSpec((1, tiles, 1, rows, width), near_map),
            ]
            + [pl.BlockSpec(memory_space=pltpu.VMEM)] * 5,
            out_specs=[
                pl.BlockSpec((1, 4, rows, width), given_map),
                pl.BlockSpec((1, 4, rows, width), kept_map),
            ],
            scratch_shapes=[pltpu.VMEM((depth // 2, width), jnp.bfloat16)] * 2,
        ),
        out_shape=[jax.ShapeDtypeStruct((2, 4, rows, width), jnp.float32)] * 2,
        compiler_params=pltpu.CompilerParams(vmem_limit_bytes=36 * 1024 * 1024),
        cost_estimate=pl.CostEstimate(
            flops=3 * total * depth * width,
            bytes_accessed=4 * total * (depth // 2 + 2 * width),
            transcendentals=0,
        ),
    )(
        where,
        ainv.reshape(2, 4, 2, rows, depth),
        near.reshape(2, 4, 2, rows, 2 * width),
        *pieces,
    )


def fence(*arrays):
    return lax.optimization_barrier(arrays)


def reduce_to_owner(kept, came):
    part = lambda dz, by: kept[dz, by] + came[dz, by]
    up_far = shift(part(0, 2), "y", 1)
    down_far = shift(part(1, 2), "y", -1)
    up_second = shift(part(1, 1), "y", 1)
    down_first = shift(part(0, 3), "y", -1)
    up_first = shift(part(0, 1) + up_far, "y", 1)
    down_second = shift(part(1, 3) + down_far, "y", -1)
    second = part(1, 0) + up_second + down_second
    across = shift(second, "zl", 1)
    return part(0, 0) + up_first + down_first + across


def sum_diag(terms, index):
    rows, width = terms.shape[0] // 128, terms.shape[1]
    terms = terms.reshape(16, 4, 2, rows, width)
    at = lambda array, axis, i: lax.dynamic_index_in_dim(array, i, axis, keepdims=False)
    terms = at(terms, 2, index["core"]) + shift(at(terms, 2, 1 - index["core"]), "core", 1)
    total = at(terms, 1, index["y"])
    for by in (1, 3, 2):
        total = total + shift(at(terms, 1, (index["y"] + by) % 4), "y", by)
    return jnp.sum(lax.all_to_all(total, ("zh", "x", "zl"), 0, 0, tiled=True), axis=0)


def expand_local(mask, block_rows, supernode):
    count = mask.shape[0]
    full = jnp.broadcast_to(
        mask.astype(jnp.float32)[:, None, :, None], (count, block_rows, 2, supernode)
    )
    return full.reshape(count * block_rows, 2 * supernode)


def local(ainv, lpanel, dinv, lmask, hrows, hmask, pole_weight):
    rows_local = lpanel.shape[0]
    supernode = lpanel.shape[1] // 2
    block_rows = rows_local // lmask.shape[0]
    index = {axis: lax.axis_index(axis) for axis in AXES}
    where = jnp.stack([index[axis] for axis in AXES]).astype(jnp.int32)
    pattern = expand_local(lmask, block_rows, supernode)
    lmasked = lpanel * pattern
    half = rows_local // 2
    (mine,) = fence(to_slabs(lmasked))
    left, right, across = fence(shift(mine, "x", 1), shift(mine, "x", -1), shift(mine, "zh", 1))
    top, bottom = fence(shift(left[:half], "x", 1), shift(right[half:], "x", -1))
    near = near_product(ainv, (mine, right, left, top, bottom), where)
    near, *others = fence(
        near,
        shift(across, "x", -1),
        shift(across, "x", 1),
        shift(top, "zh", 1),
        shift(bottom, "zh", 1),
    )
    others = (across, *others)
    given0, kept0 = fence(*far_product(ainv, near, others, where, 0))
    given1, kept1, came0 = fence(
        *far_product(ainv, near, others, where, 1), shift(given0, "core", 1)
    )
    owned = (reduce_to_owner(kept0, came0), reduce_to_owner(kept1, shift(given1, "core", 1)))
    terms = [
        lax.dot_general(
            lmasked[:, s * supernode : (s + 1) * supernode],
            owned[s],
            (((0,), (0,)), ((), ())),
            precision=lax.Precision.HIGHEST,
            preferred_element_type=jnp.float32,
        )
        for s in range(2)
    ]
    diaginv = dinv + sum_diag(jnp.concatenate(terms, axis=0), index)
    offdiag = -jnp.concatenate(owned, axis=1) * pattern
    hpattern = expand_local(hmask, block_rows, supernode)
    energy = pole_weight[0] * jnp.sum(hrows * hpattern * offdiag, axis=1)
    return (offdiag, diaginv, energy)


def solution(mesh):
    split_mesh = Mesh(mesh.devices.reshape(*SIZES), AXES)
    rows = P(AXES, None)
    return jax.shard_map(
        local,
        mesh=split_mesh,
        in_specs=(P(("zh", "x"), ("zl", "y", "core")), rows, rows, rows, rows, rows, P()),
        out_specs=(rows, rows, P(AXES)),
        check_vma=False,
    )
```

```python
import functools

import jax
import jax.numpy as jnp
from jax import lax
from jax.experimental import pallas as pl
from jax.experimental.pallas import tpu as pltpu
from jax.sharding import Mesh
from jax.sharding import PartitionSpec as P

AXES = ("zh", "x", "zl", "y", "core")
SIZES = (2, 4, 2, 4, 2)


def shift(array, axis, by):
    size = lax.axis_size(axis)
    return lax.ppermute(array, axis, [(i, (i + by) % size) for i in range(size)])


def to_slabs(array):
    pairs = []
    for zh in range(2):
        for x in range(4):
            for zl in range(2):
                for y in range(4):
                    for core in range(2):
                        source = (((zh * 4 + x) * 2 + zl) * 4 + y) * 2 + core
                        to_x = (x + y % 2 * 2 + core) % 4
                        target = (((y // 2 * 4 + to_x) * 2 + zh) * 4 + x) * 2 + zl
                        pairs.append((source, target))
    return lax.ppermute(array, AXES, pairs)


def split(value):
    high = value.astype(jnp.bfloat16)
    low = (value - high.astype(jnp.float32)).astype(jnp.bfloat16)
    return high, low


def load_pieces(where, pieces, columns, high_ref, low_ref):
    rows = pieces[0].shape[0]
    start = lambda by: lax.rem(where[1] + by - where[3] + 4, 4) * rows
    places = (start(0), start(1), start(3), start(2), start(2) + rows // 2)
    for piece, place in zip(pieces, places):
        at = pl.ds(pl.multiple_of(place, 32), piece.shape[0])
        high_ref[at, :], low_ref[at, :] = split(piece[:, columns])


def three_products(a, high_ref, low_ref):
    high, low = split(a)
    dot = functools.partial(jnp.dot, preferred_element_type=jnp.float32)
    return dot(low, high_ref[...]) + dot(high, low_ref[...]) + dot(high, high_ref[...])


def near_kernel(where, a_ref, *refs):
    pieces, out_ref, high_ref, low_ref = refs[:5], *refs[5:]

    @pl.when(pl.program_id(0) == 0)
    def _():
        load_pieces(where, pieces, slice(None), high_ref, low_ref)

    out_ref[...] = three_products(a_ref[...], high_ref, low_ref)


def near_product(ainv, pieces, where):
    total, depth = ainv.shape
    rows, width = pieces[0].shape
    tile = 2 * rows
    return pl.pallas_call(
        near_kernel,
        grid_spec=pltpu.PrefetchScalarGridSpec(
            num_scalar_prefetch=1,
            grid=(total // tile,),
            in_specs=[pl.BlockSpec((tile, depth // 2), lambda i, where: (i, where[0]))]
            + [pl.BlockSpec(memory_space=pltpu.VMEM)] * 5,
            out_specs=pl.BlockSpec((tile, width), lambda i, where: (i, 0)),
            scratch_shapes=[pltpu.VMEM((depth // 2, width), jnp.bfloat16)] * 2,
        ),
        out_shape=pltpu.HBM((total, width), jnp.float32),
        compiler_params=pltpu.CompilerParams(vmem_limit_bytes=36 * 1024 * 1024),
        cost_estimate=pl.CostEstimate(
            flops=3 * total * depth * width,
            bytes_accessed=4 * total * (depth // 2 + width),
            transcendentals=0,
        ),
    )(where, ainv, *pieces)


def far_kernel(columns, where, a_ref, near_ref, *refs):
    pieces, given_ref, kept_ref, high_ref, low_ref = refs[:5], *refs[5:]
    half, part = pl.program_id(0), pl.program_id(2)

    @pl.when((half == 0) & (pl.program_id(1) == 0) & (part == 0))
    def _():
        load_pieces(where, pieces, columns, high_ref, low_ref)

    tiles, tile_rows, depth = a_ref.shape[1], a_ref.shape[3], a_ref.shape[4]
    total = three_products(a_ref[...].reshape(tiles * tile_rows, depth), high_ref, low_ref)
    total = total + near_ref[...].reshape(total.shape)
    for which, out_ref in enumerate((given_ref, kept_ref)):

        @pl.when(half == which)
        def _():
            for tile in range(tiles):
                by = lax.rem(part * tiles + tile - where[3] + 4, 4)
                out_ref[0, by] = total[tile * tile_rows : (tile + 1) * tile_rows]


def far_product(ainv, near, pieces, where, supernode):
    total, depth = ainv.shape
    rows, width = pieces[0].shape[0], pieces[0].shape[1] // 2
    tiles = 2

    def rows_of(half, dz, part, where):
        core = jnp.bitwise_xor(where[4], 1 - half)
        return jnp.bitwise_xor(where[2], dz), part, core, 0

    def a_map(half, dz, part, where):
        return *rows_of(half, dz, part, where), 1 - where[0]

    def near_map(half, dz, part, where):
        return *rows_of(half, dz, part, where), supernode

    def given_map(half, dz, part, where):
        return jnp.maximum(half, dz), 0, 0, 0

    def kept_map(half, dz, part, where):
        return half * dz, 0, 0, 0

    columns = slice(supernode * width, (supernode + 1) * width)
    return pl.pallas_call(
        functools.partial(far_kernel, columns),
        grid_spec=pltpu.PrefetchScalarGridSpec(
            num_scalar_prefetch=1,
            grid=(2, 2, 4 // tiles),
            in_specs=[
                pl.BlockSpec((1, tiles, 1, rows, depth // 2), a_map),
                pl.BlockSpec((1, tiles, 1, rows, width), near_map),
            ]
            + [pl.BlockSpec(memory_space=pltpu.VMEM)] * 5,
            out_specs=[
                pl.BlockSpec((1, 4, rows, width), given_map),
                pl.BlockSpec((1, 4, rows, width), kept_map),
            ],
            scratch_shapes=[pltpu.VMEM((depth // 2, width), jnp.bfloat16)] * 2,
        ),
        out_shape=[jax.ShapeDtypeStruct((2, 4, rows, width), jnp.float32)] * 2,
        compiler_params=pltpu.CompilerParams(vmem_limit_bytes=36 * 1024 * 1024),
        cost_estimate=pl.CostEstimate(
            flops=3 * total * depth * width,
            bytes_accessed=4 * total * (depth // 2 + 2 * width),
            transcendentals=0,
        ),
    )(
        where,
        ainv.reshape(2, 4, 2, rows, depth),
        near.reshape(2, 4, 2, rows, 2 * width),
        *pieces,
    )


def fence(*arrays):
    return lax.optimization_barrier(arrays)


def both_ways(up, down):
    return shift(up, "y", 1), shift(down, "y", -1)


def reduce_y_first(part):
    up_far, down_far = both_ways(part[0, 2], part[1, 2])
    up_second, down_first = both_ways(part[1, 1], part[0, 3])
    up_first, down_second = both_ways(part[0, 1] + up_far, part[1, 3] + down_far)
    return part[0, 0] + up_first + down_first, part[1, 0] + up_second + down_second


def diag_term(panel, rows):
    return lax.dot_general(
        panel,
        rows,
        (((0,), (0,)), ((), ())),
        precision=lax.Precision.HIGHEST,
        preferred_element_type=jnp.float32,
    )


def sum_diag(terms, index):
    terms = terms.reshape(64, 2, terms.shape[0] // 128, terms.shape[1])
    at = lambda i: lax.dynamic_index_in_dim(terms, i, 1, keepdims=False)
    terms = at(index["core"]) + shift(at(1 - index["core"]), "core", 1)
    return jnp.sum(lax.all_to_all(terms, ("zh", "x", "zl", "y"), 0, 0, tiled=True), axis=0)


def expand_local(mask, block_rows, supernode):
    count = mask.shape[0]
    full = jnp.broadcast_to(
        mask.astype(jnp.float32)[:, None, :, None], (count, block_rows, 2, supernode)
    )
    return full.reshape(count * block_rows, 2 * supernode)


def local(ainv, lpanel, dinv, lmask, hrows, hmask, pole_weight):
    rows_local = lpanel.shape[0]
    supernode = lpanel.shape[1] // 2
    block_rows = rows_local // lmask.shape[0]
    index = {axis: lax.axis_index(axis) for axis in AXES}
    where = jnp.stack([index[axis] for axis in AXES]).astype(jnp.int32)
    pattern = expand_local(lmask, block_rows, supernode)
    lmasked = lpanel * pattern
    half = rows_local // 2
    (mine,) = fence(to_slabs(lmasked))
    left, right, across = fence(shift(mine, "x", 1), shift(mine, "x", -1), shift(mine, "zh", 1))
    top, bottom = fence(shift(left[:half], "x", 1), shift(right[half:], "x", -1))
    near = near_product(ainv, (mine, right, left, top, bottom), where)
    near, *others = fence(
        near,
        shift(across, "x", -1),
        shift(across, "x", 1),
        shift(top, "zh", 1),
        shift(bottom, "zh", 1),
    )
    others = (across, *others)
    given0, kept0, over = fence(*far_product(ainv, near, others, where, 0), lmasked)
    over = shift(over, "zl", 1)
    given1, kept1, came0 = fence(
        *far_product(ainv, near, others, where, 1), shift(given0, "core", 1)
    )
    panels = jnp.concatenate([lmasked, over])
    owned, terms = [], []
    for s, (kept, came) in enumerate(((kept0, came0), (kept1, shift(given1, "core", 1)))):
        here, there = reduce_y_first(kept + came)
        owned.append(here + shift(there, "zl", 1))
        panel = panels[:, s * supernode : (s + 1) * supernode]
        terms.append(diag_term(panel, jnp.concatenate([here, there])))
    diaginv = dinv + sum_diag(jnp.concatenate(terms, axis=0), index)
    offdiag = -jnp.concatenate(owned, axis=1) * pattern
    hpattern = expand_local(hmask, block_rows, supernode)
    energy = pole_weight[0] * jnp.sum(hrows * hpattern * offdiag, axis=1)
    return (offdiag, diaginv, energy)


def solution(mesh):
    split_mesh = Mesh(mesh.devices.reshape(*SIZES), AXES)
    rows = P(AXES, None)
    return jax.shard_map(
        local,
        mesh=split_mesh,
        in_specs=(P(("zh", "x"), ("zl", "y", "core")), rows, rows, rows, rows, rows, P()),
        out_specs=(rows, rows, P(AXES)),
        check_vma=False,
    )
```

```python
import functools

import jax
import jax.numpy as jnp
from jax import lax
from jax.experimental import pallas as pl
from jax.experimental.pallas import tpu as pltpu
from jax.sharding import Mesh
from jax.sharding import PartitionSpec as P

AXES = ("zh", "x", "zl", "y", "core")
SIZES = (2, 4, 2, 4, 2)


def shift(array, axis, by):
    size = lax.axis_size(axis)
    return lax.ppermute(array, axis, [(i, (i + by) % size) for i in range(size)])


def to_slabs(array):
    pairs = []
    for zh in range(2):
        for x in range(4):
            for zl in range(2):
                for y in range(4):
                    for core in range(2):
                        source = (((zh * 4 + x) * 2 + zl) * 4 + y) * 2 + core
                        to_x = (x + y % 2 * 2 + core) % 4
                        target = (((y // 2 * 4 + to_x) * 2 + zh) * 4 + x) * 2 + zl
                        pairs.append((source, target))
    return lax.ppermute(array, AXES, pairs)


def split(value):
    high = value.astype(jnp.bfloat16)
    low = (value - high.astype(jnp.float32)).astype(jnp.bfloat16)
    return high, low


def load_pieces(where, pieces, columns, high_ref, low_ref):
    rows = high_ref.shape[0] // 4
    done = 0
    for piece in pieces:
        by, part = (0, 1, 3, 2)[done // rows], done % rows
        place = lax.rem(where[1] + by - where[3] + 4, 4) * rows + part
        at = pl.ds(pl.multiple_of(place, 32), piece.shape[0])
        high_ref[at, :], low_ref[at, :] = split(piece[:, columns])
        done += piece.shape[0]


def three_products(a, high_ref, low_ref):
    high, low = split(a)
    dot = functools.partial(jnp.dot, preferred_element_type=jnp.float32)
    return dot(low, high_ref[...]) + dot(high, low_ref[...]) + dot(high, high_ref[...])


def near_kernel(where, a_ref, *refs):
    pieces, out_ref, high_ref, low_ref = refs[:-3], *refs[-3:]

    @pl.when(pl.program_id(0) == 0)
    def _():
        load_pieces(where, pieces, slice(None), high_ref, low_ref)

    out_ref[...] = three_products(a_ref[...], high_ref, low_ref)


def near_product(ainv, pieces, where):
    total, depth = ainv.shape
    width = pieces[0].shape[1]
    tile = total // 8
    return pl.pallas_call(
        near_kernel,
        grid_spec=pltpu.PrefetchScalarGridSpec(
            num_scalar_prefetch=1,
            grid=(total // tile,),
            in_specs=[pl.BlockSpec((tile, depth // 2), lambda i, where: (i, where[0]))]
            + [pl.BlockSpec(memory_space=pltpu.VMEM)] * len(pieces),
            out_specs=pl.BlockSpec((tile, width), lambda i, where: (i, 0)),
            scratch_shapes=[pltpu.VMEM((depth // 2, width), jnp.bfloat16)] * 2,
        ),
        out_shape=pltpu.HBM((total, width), jnp.float32),
        compiler_params=pltpu.CompilerParams(vmem_limit_bytes=36 * 1024 * 1024),
        cost_estimate=pl.CostEstimate(
            flops=3 * total * depth * width,
            bytes_accessed=4 * total * (depth // 2 + width),
            transcendentals=0,
        ),
    )(where, ainv, *pieces)


def far_kernel(columns, where, a_ref, near_ref, *refs):
    pieces, given_ref, kept_ref, high_ref, low_ref = refs[:5], *refs[5:]
    half, part = pl.program_id(0), pl.program_id(2)

    @pl.when((half == 0) & (pl.program_id(1) == 0) & (part == 0))
    def _():
        load_pieces(where, pieces, columns, high_ref, low_ref)

    tiles, tile_rows, depth = a_ref.shape[1], a_ref.shape[3], a_ref.shape[4]
    total = three_products(a_ref[...].reshape(tiles * tile_rows, depth), high_ref, low_ref)
    total = total + near_ref[...].reshape(total.shape)
    for which, out_ref in enumerate((given_ref, kept_ref)):

        @pl.when(half == which)
        def _():
            for tile in range(tiles):
                by = lax.rem(part * tiles + tile - where[3] + 4, 4)
                out_ref[0, by] = total[tile * tile_rows : (tile + 1) * tile_rows]


def far_product(ainv, near, pieces, where, supernode):
    total, depth = ainv.shape
    rows, width = pieces[0].shape[0], pieces[0].shape[1] // 2
    tiles = 2

    def rows_of(half, dz, part, where):
        core = jnp.bitwise_xor(where[4], 1 - half)
        return jnp.bitwise_xor(where[2], dz), part, core, 0

    def a_map(half, dz, part, where):
        return *rows_of(half, dz, part, where), 1 - where[0]

    def near_map(half, dz, part, where):
        return *rows_of(half, dz, part, where), supernode

    def given_map(half, dz, part, where):
        return jnp.maximum(half, dz), 0, 0, 0

    def kept_map(half, dz, part, where):
        return half * dz, 0, 0, 0

    columns = slice(supernode * width, (supernode + 1) * width)
    return pl.pallas_call(
        functools.partial(far_kernel, columns),
        grid_spec=pltpu.PrefetchScalarGridSpec(
            num_scalar_prefetch=1,
            grid=(2, 2, 4 // tiles),
            in_specs=[
                pl.BlockSpec((1, tiles, 1, rows, depth // 2), a_map),
                pl.BlockSpec((1, tiles, 1, rows, width), near_map),
            ]
            + [pl.BlockSpec(memory_space=pltpu.VMEM)] * 5,
            out_specs=[
                pl.BlockSpec((1, 4, rows, width), given_map),
                pl.BlockSpec((1, 4, rows, width), kept_map),
            ],
            scratch_shapes=[pltpu.VMEM((depth // 2, width), jnp.bfloat16)] * 2,
        ),
        out_shape=[jax.ShapeDtypeStruct((2, 4, rows, width), jnp.float32)] * 2,
        compiler_params=pltpu.CompilerParams(vmem_limit_bytes=36 * 1024 * 1024),
        cost_estimate=pl.CostEstimate(
            flops=3 * total * depth * width,
            bytes_accessed=4 * total * (depth // 2 + 2 * width),
            transcendentals=0,
        ),
    )(
        where,
        ainv.reshape(2, 4, 2, rows, depth),
        near.reshape(2, 4, 2, rows, 2 * width),
        *pieces,
    )


def fence(*arrays):
    return lax.optimization_barrier(arrays)


def both_ways(up, down):
    return shift(up, "y", 1), shift(down, "y", -1)


def reduce_y_first(part):
    up_far, down_far = both_ways(part[0, 2], part[1, 2])
    up_second, down_first = both_ways(part[1, 1], part[0, 3])
    up_first, down_second = both_ways(part[0, 1] + up_far, part[1, 3] + down_far)
    return part[0, 0] + up_first + down_first, part[1, 0] + up_second + down_second


def diag_term(panel, rows):
    return lax.dot_general(
        panel,
        rows,
        (((0,), (0,)), ((), ())),
        precision=lax.Precision.HIGHEST,
        preferred_element_type=jnp.float32,
    )


def sum_diag(terms, index):
    terms = terms.reshape(64, 2, terms.shape[0] // 128, terms.shape[1])
    at = lambda i: lax.dynamic_index_in_dim(terms, i, 1, keepdims=False)
    terms = at(index["core"]) + shift(at(1 - index["core"]), "core", 1)
    return jnp.sum(lax.all_to_all(terms, ("zh", "x", "zl", "y"), 0, 0, tiled=True), axis=0)


def expand_local(mask, block_rows, supernode):
    count = mask.shape[0]
    full = jnp.broadcast_to(
        mask.astype(jnp.float32)[:, None, :, None], (count, block_rows, 2, supernode)
    )
    return full.reshape(count * block_rows, 2 * supernode)


def local(ainv, lpanel, dinv, lmask, hrows, hmask, pole_weight):
    rows_local = lpanel.shape[0]
    supernode = lpanel.shape[1] // 2
    block_rows = rows_local // lmask.shape[0]
    index = {axis: lax.axis_index(axis) for axis in AXES}
    where = jnp.stack([index[axis] for axis in AXES]).astype(jnp.int32)
    pattern = expand_local(lmask, block_rows, supernode)
    lmasked = lpanel * pattern
    half = rows_local // 2
    mine_top, mine_low = to_slabs(lmasked[:half]), to_slabs(lmasked[half:])
    (mine_top,) = fence(mine_top)
    left_top, right_top, mine_low = fence(
        shift(mine_top, "x", 1), shift(mine_top, "x", -1), mine_low
    )
    left_low, right_low = shift(mine_low, "x", 1), shift(mine_low, "x", -1)
    across = shift(jnp.concatenate([mine_top, mine_low]), "zh", 1)
    left_low, right_low = fence(left_low, right_low)
    top, bottom, across = fence(shift(left_top, "x", 1), shift(right_low, "x", -1), across)
    own = (mine_top, mine_low, right_top, right_low, left_top, left_low, top, bottom)
    near = near_product(ainv, own, where)
    near, *others = fence(
        near,
        shift(across, "x", -1),
        shift(across, "x", 1),
        shift(top, "zh", 1),
        shift(bottom, "zh", 1),
    )
    others = (across, *others)
    given0, kept0, over = fence(*far_product(ainv, near, others, where, 0), lmasked)
    over = shift(over, "zl", 1)
    given1, kept1, came0 = fence(
        *far_product(ainv, near, others, where, 1), shift(given0, "core", 1)
    )
    panels = jnp.concatenate([lmasked, over])
    owned, terms = [], []
    for s, (kept, came) in enumerate(((kept0, came0), (kept1, shift(given1, "core", 1)))):
        here, there = reduce_y_first(kept + came)
        owned.append(here + shift(there, "zl", 1))
        panel = panels[:, s * supernode : (s + 1) * supernode]
        terms.append(diag_term(panel, jnp.concatenate([here, there])))
    diaginv = dinv + sum_diag(jnp.concatenate(terms, axis=0), index)
    offdiag = -jnp.concatenate(owned, axis=1) * pattern
    hpattern = expand_local(hmask, block_rows, supernode)
    energy = pole_weight[0] * jnp.sum(hrows * hpattern * offdiag, axis=1)
    return (offdiag, diaginv, energy)


def solution(mesh):
    split_mesh = Mesh(mesh.devices.reshape(*SIZES), AXES)
    rows = P(AXES, None)
    return jax.shard_map(
        local,
        mesh=split_mesh,
        in_specs=(P(("zh", "x"), ("zl", "y", "core")), rows, rows, rows, rows, rows, P()),
        out_specs=(rows, rows, P(AXES)),
        check_vma=False,
    )
```

```python
import functools

import jax
import jax.numpy as jnp
from jax import lax
from jax.experimental import pallas as pl
from jax.experimental.pallas import tpu as pltpu
from jax.sharding import Mesh
from jax.sharding import PartitionSpec as P

AXES = ("zh", "x", "zl", "y", "core")
SIZES = (2, 4, 2, 4, 2)


def shift(array, axis, by):
    size = lax.axis_size(axis)
    return lax.ppermute(array, axis, [(i, (i + by) % size) for i in range(size)])


def to_slabs(array):
    pairs = []
    for zh in range(2):
        for x in range(4):
            for zl in range(2):
                for y in range(4):
                    for core in range(2):
                        source = (((zh * 4 + x) * 2 + zl) * 4 + y) * 2 + core
                        to_x = (x + y % 2 * 2 + core) % 4
                        target = (((y // 2 * 4 + to_x) * 2 + zh) * 4 + x) * 2 + zl
                        pairs.append((source, target))
    return lax.ppermute(array, AXES, pairs)


def split(value):
    high = value.astype(jnp.bfloat16)
    low = (value - high.astype(jnp.float32)).astype(jnp.bfloat16)
    return high, low


def load_pieces(where, pieces, columns, high_ref, low_ref):
    rows = high_ref.shape[0] // 4
    done = 0
    for piece in pieces:
        by, part = (0, 1, 3, 2)[done // rows], done % rows
        place = lax.rem(where[1] + by - where[3] + 4, 4) * rows + part
        at = pl.ds(pl.multiple_of(place, 32), piece.shape[0])
        high_ref[at, :], low_ref[at, :] = split(piece[:, columns])
        done += piece.shape[0]


def three_products(a, high_ref, low_ref):
    high, low = split(a)
    dot = functools.partial(jnp.dot, preferred_element_type=jnp.float32)
    return dot(low, high_ref[...]) + dot(high, low_ref[...]) + dot(high, high_ref[...])


def near_kernel(where, a_ref, *refs):
    pieces, out_ref, high_ref, low_ref = refs[:-3], *refs[-3:]

    @pl.when(pl.program_id(0) == 0)
    def _():
        load_pieces(where, pieces, slice(None), high_ref, low_ref)

    out_ref[...] = three_products(a_ref[...], high_ref, low_ref)


def near_product(ainv, pieces, where):
    total, depth = ainv.shape
    width = pieces[0].shape[1]
    tile = total // 8
    return pl.pallas_call(
        near_kernel,
        grid_spec=pltpu.PrefetchScalarGridSpec(
            num_scalar_prefetch=1,
            grid=(total // tile,),
            in_specs=[pl.BlockSpec((tile, depth // 2), lambda i, where: (i, where[0]))]
            + [pl.BlockSpec(memory_space=pltpu.VMEM)] * len(pieces),
            out_specs=pl.BlockSpec((tile, width), lambda i, where: (i, 0)),
            scratch_shapes=[pltpu.VMEM((depth // 2, width), jnp.bfloat16)] * 2,
        ),
        out_shape=pltpu.HBM((total, width), jnp.float32),
        compiler_params=pltpu.CompilerParams(vmem_limit_bytes=36 * 1024 * 1024),
        cost_estimate=pl.CostEstimate(
            flops=3 * total * depth * width,
            bytes_accessed=4 * total * (depth // 2 + width),
            transcendentals=0,
        ),
    )(where, ainv, *pieces)


def far_kernel(columns, where, a_ref, near_ref, *refs):
    pieces, given_ref, kept_ref, high_ref, low_ref = refs[:5], *refs[5:]
    half, part = pl.program_id(0), pl.program_id(2)

    @pl.when((half == 0) & (pl.program_id(1) == 0) & (part == 0))
    def _():
        load_pieces(where, pieces, columns, high_ref, low_ref)

    tiles, tile_rows, depth = a_ref.shape[1], a_ref.shape[3], a_ref.shape[4]
    total = three_products(a_ref[...].reshape(tiles * tile_rows, depth), high_ref, low_ref)
    total = total + near_ref[...].reshape(total.shape)
    for which, out_ref in enumerate((given_ref, kept_ref)):

        @pl.when(half == which)
        def _():
            for tile in range(tiles):
                by = lax.rem(part * tiles + tile - where[3] + 4, 4)
                out_ref[0, by] = total[tile * tile_rows : (tile + 1) * tile_rows]


def far_product(ainv, near, pieces, where, supernode):
    total, depth = ainv.shape
    rows, width = pieces[0].shape[0], pieces[0].shape[1] // 2
    tiles = 2

    def rows_of(half, dz, part, where):
        core = jnp.bitwise_xor(where[4], 1 - half)
        return jnp.bitwise_xor(where[2], dz), part, core, 0

    def a_map(half, dz, part, where):
        return *rows_of(half, dz, part, where), 1 - where[0]

    def near_map(half, dz, part, where):
        return *rows_of(half, dz, part, where), supernode

    def given_map(half, dz, part, where):
        return jnp.maximum(half, dz), 0, 0, 0

    def kept_map(half, dz, part, where):
        return half * dz, 0, 0, 0

    columns = slice(supernode * width, (supernode + 1) * width)
    return pl.pallas_call(
        functools.partial(far_kernel, columns),
        grid_spec=pltpu.PrefetchScalarGridSpec(
            num_scalar_prefetch=1,
            grid=(2, 2, 4 // tiles),
            in_specs=[
                pl.BlockSpec((1, tiles, 1, rows, depth // 2), a_map),
                pl.BlockSpec((1, tiles, 1, rows, width), near_map),
            ]
            + [pl.BlockSpec(memory_space=pltpu.VMEM)] * 5,
            out_specs=[
                pl.BlockSpec((1, 4, rows, width), given_map),
                pl.BlockSpec((1, 4, rows, width), kept_map),
            ],
            scratch_shapes=[pltpu.VMEM((depth // 2, width), jnp.bfloat16)] * 2,
        ),
        out_shape=[jax.ShapeDtypeStruct((2, 4, rows, width), jnp.float32)] * 2,
        compiler_params=pltpu.CompilerParams(vmem_limit_bytes=36 * 1024 * 1024),
        cost_estimate=pl.CostEstimate(
            flops=3 * total * depth * width,
            bytes_accessed=4 * total * (depth // 2 + 2 * width),
            transcendentals=0,
        ),
    )(
        where,
        ainv.reshape(2, 4, 2, rows, depth),
        near.reshape(2, 4, 2, rows, 2 * width),
        *pieces,
    )


def fence(*arrays):
    return lax.optimization_barrier(arrays)


def both_ways(up, down):
    return shift(up, "y", 1), shift(down, "y", -1)


def reduce_y_first(part):
    up_far, down_far = both_ways(part[0, 2], part[1, 2])
    up_second, down_first = both_ways(part[1, 1], part[0, 3])
    up_first, down_second = both_ways(part[0, 1] + up_far, part[1, 3] + down_far)
    return part[0, 0] + up_first + down_first, part[1, 0] + up_second + down_second


def diag_term(panel, rows):
    return lax.dot_general(
        panel,
        rows,
        (((0,), (0,)), ((), ())),
        precision=lax.Precision.HIGH,
        preferred_element_type=jnp.float32,
    )


def sum_diag(terms, index):
    terms = terms.reshape(64, 2, terms.shape[0] // 128, terms.shape[1])
    at = lambda i: lax.dynamic_index_in_dim(terms, i, 1, keepdims=False)
    terms = at(index["core"]) + shift(at(1 - index["core"]), "core", 1)
    return jnp.sum(lax.all_to_all(terms, ("zh", "x", "zl", "y"), 0, 0, tiled=True), axis=0)


def expand_local(mask, block_rows, supernode):
    count = mask.shape[0]
    full = jnp.broadcast_to(
        mask.astype(jnp.float32)[:, None, :, None], (count, block_rows, 2, supernode)
    )
    return full.reshape(count * block_rows, 2 * supernode)


def local(ainv, lpanel, dinv, lmask, hrows, hmask, pole_weight):
    rows_local = lpanel.shape[0]
    supernode = lpanel.shape[1] // 2
    block_rows = rows_local // lmask.shape[0]
    index = {axis: lax.axis_index(axis) for axis in AXES}
    where = jnp.stack([index[axis] for axis in AXES]).astype(jnp.int32)
    pattern = expand_local(lmask, block_rows, supernode)
    lmasked = lpanel * pattern
    half = rows_local // 2
    mine_top = to_slabs(lpanel[:half] * pattern[:half])
    mine_low = to_slabs(lpanel[half:] * pattern[half:])
    (mine_top,) = fence(mine_top)
    left_top, right_top, mine_low = fence(
        shift(mine_top, "x", 1), shift(mine_top, "x", -1), mine_low
    )
    left_low, right_low = shift(mine_low, "x", 1), shift(mine_low, "x", -1)
    across = shift(jnp.concatenate([mine_top, mine_low]), "zh", 1)
    left_low, right_low = fence(left_low, right_low)
    top, bottom, across = fence(shift(left_top, "x", 1), shift(right_low, "x", -1), across)
    own = (mine_top, mine_low, right_top, right_low, left_top, left_low, top, bottom)
    near = near_product(ainv, own, where)
    near, *others = fence(
        near,
        shift(across, "x", -1),
        shift(across, "x", 1),
        shift(top, "zh", 1),
        shift(bottom, "zh", 1),
    )
    others = (across, *others)
    given0, kept0, over = fence(*far_product(ainv, near, others, where, 0), lmasked)
    over = shift(over, "zl", 1)
    given1, kept1, came0 = fence(
        *far_product(ainv, near, others, where, 1), shift(given0, "core", 1)
    )
    panels = jnp.concatenate([lmasked, over])
    owned, terms = [], []
    for s, (kept, came) in enumerate(((kept0, came0), (kept1, shift(given1, "core", 1)))):
        here, there = reduce_y_first(kept + came)
        owned.append(here + shift(there, "zl", 1))
        panel = panels[:, s * supernode : (s + 1) * supernode]
        terms.append(diag_term(panel, jnp.concatenate([here, there])))
    diaginv = dinv + sum_diag(jnp.concatenate(terms, axis=0), index)
    offdiag = -jnp.concatenate(owned, axis=1) * pattern
    hpattern = expand_local(hmask, block_rows, supernode)
    energy = pole_weight[0] * jnp.sum(hrows * hpattern * offdiag, axis=1)
    return (offdiag, diaginv, energy)


def solution(mesh):
    split_mesh = Mesh(mesh.devices.reshape(*SIZES), AXES)
    rows = P(AXES, None)
    return jax.shard_map(
        local,
        mesh=split_mesh,
        in_specs=(P(("zh", "x"), ("zl", "y", "core")), rows, rows, rows, rows, rows, P()),
        out_specs=(rows, rows, P(AXES)),
        check_vma=False,
    )
```

```python
import functools

import jax
import jax.numpy as jnp
from jax import lax
from jax.experimental import pallas as pl
from jax.experimental.pallas import tpu as pltpu
from jax.sharding import Mesh
from jax.sharding import PartitionSpec as P

AXES = ("zh", "x", "zl", "y", "core")
SIZES = (2, 4, 2, 4, 2)


def shift(array, axis, by):
    size = lax.axis_size(axis)
    return lax.ppermute(array, axis, [(i, (i + by) % size) for i in range(size)])


def to_slabs(array):
    pairs = []
    for zh in range(2):
        for x in range(4):
            for zl in range(2):
                for y in range(4):
                    for core in range(2):
                        source = (((zh * 4 + x) * 2 + zl) * 4 + y) * 2 + core
                        to_x = (x + y % 2 * 2 + core) % 4
                        target = (((y // 2 * 4 + to_x) * 2 + zh) * 4 + x) * 2 + zl
                        pairs.append((source, target))
    return lax.ppermute(array, AXES, pairs)


def split(value):
    high = value.astype(jnp.bfloat16)
    low = (value - high.astype(jnp.float32)).astype(jnp.bfloat16)
    return high, low


def load_pieces(where, pieces, columns, high_ref, low_ref):
    rows = high_ref.shape[0] // 4
    done = 0
    for piece in pieces:
        by, part = (0, 1, 3, 2)[done // rows], done % rows
        place = lax.rem(where[1] + by - where[3] + 4, 4) * rows + part
        at = pl.ds(pl.multiple_of(place, 32), piece.shape[0])
        high_ref[at, :], low_ref[at, :] = split(piece[:, columns])
        done += piece.shape[0]


def three_products(a, high_ref, low_ref):
    high, low = split(a)
    dot = functools.partial(jnp.dot, preferred_element_type=jnp.float32)
    return dot(low, high_ref[...]) + dot(high, low_ref[...]) + dot(high, high_ref[...])


def near_kernel(where, a_ref, *refs):
    pieces, out_ref, high_ref, low_ref = refs[:-3], *refs[-3:]

    @pl.when(pl.program_id(0) == 0)
    def _():
        load_pieces(where, pieces, slice(None), high_ref, low_ref)

    out_ref[...] = three_products(a_ref[...], high_ref, low_ref)


def near_product(ainv, pieces, where):
    total, depth = ainv.shape
    width = pieces[0].shape[1]
    tile = total // 4
    return pl.pallas_call(
        near_kernel,
        grid_spec=pltpu.PrefetchScalarGridSpec(
            num_scalar_prefetch=1,
            grid=(total // tile,),
            in_specs=[pl.BlockSpec((tile, depth // 2), lambda i, where: (i, where[0]))]
            + [pl.BlockSpec(memory_space=pltpu.VMEM)] * len(pieces),
            out_specs=pl.BlockSpec((tile, width), lambda i, where: (i, 0)),
            scratch_shapes=[pltpu.VMEM((depth // 2, width), jnp.bfloat16)] * 2,
        ),
        out_shape=pltpu.HBM((total, width), jnp.float32),
        compiler_params=pltpu.CompilerParams(vmem_limit_bytes=36 * 1024 * 1024),
        cost_estimate=pl.CostEstimate(
            flops=3 * total * depth * width,
            bytes_accessed=4 * total * (depth // 2 + width),
            transcendentals=0,
        ),
    )(where, ainv, *pieces)


def far_kernel(columns, where, a_ref, near_ref, *refs):
    pieces, given_ref, kept_ref, high_ref, low_ref = refs[:5], *refs[5:]
    half, part = pl.program_id(0), pl.program_id(2)

    @pl.when((half == 0) & (pl.program_id(1) == 0) & (part == 0))
    def _():
        load_pieces(where, pieces, columns, high_ref, low_ref)

    tiles, tile_rows, depth = a_ref.shape[1], a_ref.shape[3], a_ref.shape[4]
    total = three_products(a_ref[...].reshape(tiles * tile_rows, depth), high_ref, low_ref)
    total = total + near_ref[...].reshape(total.shape)
    for which, out_ref in enumerate((given_ref, kept_ref)):

        @pl.when(half == which)
        def _():
            for tile in range(tiles):
                by = lax.rem(part * tiles + tile - where[3] + 4, 4)
                out_ref[0, by] = total[tile * tile_rows : (tile + 1) * tile_rows]


def far_product(ainv, near, pieces, where, supernode):
    total, depth = ainv.shape
    rows, width = pieces[0].shape[0], pieces[0].shape[1] // 2
    tiles = 4

    def rows_of(half, dz, part, where):
        core = jnp.bitwise_xor(where[4], 1 - half)
        return jnp.bitwise_xor(where[2], dz), part, core, 0

    def a_map(half, dz, part, where):
        return *rows_of(half, dz, part, where), 1 - where[0]

    def near_map(half, dz, part, where):
        return *rows_of(half, dz, part, where), supernode

    def given_map(half, dz, part, where):
        return jnp.maximum(half, dz), 0, 0, 0

    def kept_map(half, dz, part, where):
        return half * dz, 0, 0, 0

    columns = slice(supernode * width, (supernode + 1) * width)
    return pl.pallas_call(
        functools.partial(far_kernel, columns),
        grid_spec=pltpu.PrefetchScalarGridSpec(
            num_scalar_prefetch=1,
            grid=(2, 2, 4 // tiles),
            in_specs=[
                pl.BlockSpec((1, tiles, 1, rows, depth // 2), a_map),
                pl.BlockSpec((1, tiles, 1, rows, width), near_map),
            ]
            + [pl.BlockSpec(memory_space=pltpu.VMEM)] * 5,
            out_specs=[
                pl.BlockSpec((1, 4, rows, width), given_map),
                pl.BlockSpec((1, 4, rows, width), kept_map),
            ],
            scratch_shapes=[pltpu.VMEM((depth // 2, width), jnp.bfloat16)] * 2,
        ),
        out_shape=[jax.ShapeDtypeStruct((2, 4, rows, width), jnp.float32)] * 2,
        compiler_params=pltpu.CompilerParams(vmem_limit_bytes=36 * 1024 * 1024),
        cost_estimate=pl.CostEstimate(
            flops=3 * total * depth * width,
            bytes_accessed=4 * total * (depth // 2 + 2 * width),
            transcendentals=0,
        ),
    )(
        where,
        ainv.reshape(2, 4, 2, rows, depth),
        near.reshape(2, 4, 2, rows, 2 * width),
        *pieces,
    )


def fence(*arrays):
    return lax.optimization_barrier(arrays)


def both_ways(up, down):
    return shift(up, "y", 1), shift(down, "y", -1)


def reduce_y_first(part):
    up_far, down_far = both_ways(part[0, 2], part[1, 2])
    up_second, down_first = both_ways(part[1, 1], part[0, 3])
    up_first, down_second = both_ways(part[0, 1] + up_far, part[1, 3] + down_far)
    return part[0, 0] + up_first + down_first, part[1, 0] + up_second + down_second


def diag_term(panel, rows):
    return lax.dot_general(
        panel,
        rows,
        (((0,), (0,)), ((), ())),
        precision=lax.Precision.HIGH,
        preferred_element_type=jnp.float32,
    )


def sum_diag(terms, index):
    terms = terms.reshape(64, 2, terms.shape[0] // 128, terms.shape[1])
    at = lambda i: lax.dynamic_index_in_dim(terms, i, 1, keepdims=False)
    terms = at(index["core"]) + shift(at(1 - index["core"]), "core", 1)
    return jnp.sum(lax.all_to_all(terms, ("zh", "x", "zl", "y"), 0, 0, tiled=True), axis=0)


def expand_local(mask, block_rows, supernode):
    count = mask.shape[0]
    full = jnp.broadcast_to(
        mask.astype(jnp.float32)[:, None, :, None], (count, block_rows, 2, supernode)
    )
    return full.reshape(count * block_rows, 2 * supernode)


def local(ainv, lpanel, dinv, lmask, hrows, hmask, pole_weight):
    rows_local = lpanel.shape[0]
    supernode = lpanel.shape[1] // 2
    block_rows = rows_local // lmask.shape[0]
    index = {axis: lax.axis_index(axis) for axis in AXES}
    where = jnp.stack([index[axis] for axis in AXES]).astype(jnp.int32)
    pattern = expand_local(lmask, block_rows, supernode)
    lmasked = lpanel * pattern
    half = rows_local // 2
    mine_top = to_slabs(lpanel[:half] * pattern[:half])
    mine_low = to_slabs(lpanel[half:] * pattern[half:])
    (mine_top,) = fence(mine_top)
    left_top, right_top, mine_low = fence(
        shift(mine_top, "x", 1), shift(mine_top, "x", -1), mine_low
    )
    left_low, right_low = shift(mine_low, "x", 1), shift(mine_low, "x", -1)
    across = shift(jnp.concatenate([mine_top, mine_low]), "zh", 1)
    left_low, right_low = fence(left_low, right_low)
    top, bottom = fence(shift(left_top, "x", 1), shift(right_low, "x", -1))
    own = (mine_top, mine_low, right_top, right_low, left_top, left_low, top, bottom)
    near = near_product(ainv, own, where)
    near, *others = fence(
        near,
        shift(across, "x", -1),
        shift(across, "x", 1),
        shift(top, "zh", 1),
        shift(bottom, "zh", 1),
    )
    others = (across, *others)
    given0, kept0, over = fence(*far_product(ainv, near, others, where, 0), lmasked)
    over = shift(over, "zl", 1)
    given1, kept1, came0 = fence(
        *far_product(ainv, near, others, where, 1), shift(given0, "core", 1)
    )
    panels = jnp.concatenate([lmasked, over])
    owned, terms = [], []
    for s, (kept, came) in enumerate(((kept0, came0), (kept1, shift(given1, "core", 1)))):
        here, there = reduce_y_first(kept + came)
        owned.append(here + shift(there, "zl", 1))
        panel = panels[:, s * supernode : (s + 1) * supernode]
        terms.append(diag_term(panel, jnp.concatenate([here, there])))
    diaginv = dinv + sum_diag(jnp.concatenate(terms, axis=0), index)
    offdiag = -jnp.concatenate(owned, axis=1) * pattern
    hpattern = expand_local(hmask, block_rows, supernode)
    energy = pole_weight[0] * jnp.sum(hrows * hpattern * offdiag, axis=1)
    return (offdiag, diaginv, energy)


def solution(mesh):
    split_mesh = Mesh(mesh.devices.reshape(*SIZES), AXES)
    rows = P(AXES, None)
    return jax.shard_map(
        local,
        mesh=split_mesh,
        in_specs=(P(("zh", "x"), ("zl", "y", "core")), rows, rows, rows, rows, rows, P()),
        out_specs=(rows, rows, P(AXES)),
        check_vma=False,
    )
```
